32 devices in a mesh: ctx: 8 (over z, x), tp: 4 (over y, core).
Axes of the slice: x: 2, y: 2, z: 4, core: 2. Of those that a mesh axis runs over, the one named last changes fastest.
Arguments:
- query_heads: bfloat16 [2048, 4096], P('ctx', 'tp'), may hold values from -10 to 10
- key_heads: bfloat16 [2048, 1024], P('ctx'), may hold values from -6 to 6
- value_heads: bfloat16 [2048, 1024], P('ctx'), may hold values from -6 to 6
- grad_rows: bfloat16 [2048, 4096], P(('ctx', 'tp')), may hold values from -6 to 6
- doc_lengths: int32 [4], replicated, may hold values from 1 to 7, 16 in all
Outputs:
- attn_out: bfloat16 [2048, 4096], P(('ctx', 'tp'))
- d_query: bfloat16 [2048, 4096], P('ctx', 'tp')
- d_key: bfloat16 [2048, 1024], P(('ctx', 'tp'))
- d_value: bfloat16 [2048, 1024], P(('ctx', 'tp'))
The draws below stay inside these ranges and needn't reach their ends.
Inputs may be any that keep to these rules, and one draw needn't show every extreme that they name: `doc_lengths`: lengths of the packed row's documents in blocks of 128 tokens, in order; they sum to 16 and one is exactly 7.
All inputs are finite; a program needn't handle non-finite values.
Results may differ from the reference program's by a relative error of at most 0.025.
Values may be sent and summed in bfloat16 or wider, within the bound.
A program may use at most 64 MiB of HBM per device.

```python
import math
import jax
import jax.numpy as jnp
import numpy as np
from jax import lax

H = 32
KVH = 8
HD = 128
BLK = 128
TOKENS = 2048
MOSTB = 7
NBLK = 16
NDOC = 4


def base_keys(key):
    normal_rows = jax.random.normal(jax.random.fold_in(key, 7), (TOKENS, KVH * HD), jnp.float32)
    return jnp.clip(normal_rows, -5.0, 5.0)


def draw_key_heads(key, part):
    return base_keys(key).astype(jnp.bfloat16)


def draw_query_heads(key, part):
    normal_rows = jax.random.normal(jax.random.fold_in(key, 8), (TOKENS, H * HD), jnp.float32)
    query_rows = jnp.clip(normal_rows, -5.0, 5.0)
    return query_rows.astype(jnp.bfloat16)


def steps_of(rng, extent, split, least, top_value):
    def one(axis_at, blocks):
        steps = jax.random.uniform(jax.random.fold_in(jax.random.fold_in(rng, 6), axis_at), (blocks,), jnp.float32, least / len(split), top_value / len(split))
        return jnp.repeat(jnp.exp(steps), extent[axis_at] // blocks).reshape((-1,) + (1,) * (len(extent) - axis_at - 1))

    loudness = one(*split[0])
    for cut in split[1:]:
        loudness = loudness * one(*cut)
    return loudness


def length_profile(count, total, most, lean):
    loads = [(1 << 20) // math.isqrt(rank ** lean) + 1 for rank in range(2, count + 1)]
    spare, counts = total - most - (count - 1), [1] * (count - 1)
    while spare > 0:
        candidates = [i for i in range(count - 1) if counts[i] < most]
        mass, budget = sum([loads[i] for i in candidates]), spare
        for i in candidates:
            more = min(most - counts[i], max(1, budget * loads[i] // mass), spare)
            counts[i] = counts[i] + more
            spare = spare - more
    return np.array([most] + counts)


def ragged(own_key, amount, total, most, lean):
    if amount == 2:
        one = jax.random.randint(own_key, (), max(1, total - most), min(most, total - 1) + 1)
        return jnp.stack([one, total - one])
    tallies = jnp.asarray(length_profile(amount, total, most, lean), jnp.int32)
    couples = (amount - 1) // 2
    donor, taker = tallies[1:1 + 2 * couples:2], tallies[2:2 + 2 * couples:2]
    slack = jnp.minimum(donor - 1, most - taker)
    moved = jax.random.randint(jax.random.fold_in(own_key, 1), (couples,), 0, 1 << 20) % (slack + 1)
    tallies = tallies.at[1:1 + 2 * couples:2].set(donor - moved).at[2:2 + 2 * couples:2].set(taker + moved)
    return tallies[jax.random.permutation(jax.random.fold_in(own_key, 2), amount)]


def centred(own_key, extent, width, most, cuts=(), held_as=jnp.bfloat16):
    values = jax.random.normal(own_key, extent, jnp.float32) * width
    if len(cuts) > 0:
        values = steps_of(own_key, extent, cuts, -0.22, 0.18) * values
    return jnp.clip(values, min=-most, max=most).astype(held_as)


def setup_inputs(seed: int = 0) -> dict:
    seeds = jax.random.split(jax.random.key(seed), 6)
    query_heads = draw_query_heads(jax.random.fold_in(seeds[5], 71), 0)
    key_heads = draw_key_heads(jax.random.fold_in(seeds[5], 71), 0)
    value_heads = centred(seeds[2], (TOKENS, KVH * HD), 1.0, 6.0, ((0, 8),))
    grad_rows = centred(seeds[3], (TOKENS, H * HD), 1.0, 6.0, ((0, 32),))
    doc_lengths = ragged(seeds[4], NDOC, NBLK, MOSTB, 0).astype(jnp.int32)
    return dict(query_heads=query_heads, key_heads=key_heads, value_heads=value_heads, grad_rows=grad_rows, doc_lengths=doc_lengths)


def reference(query_heads, key_heads, value_heads, grad_rows, doc_lengths):
    per_kv = H // KVH
    margin = (MOSTB - 1) * BLK
    window = MOSTB * BLK
    scaling = 1.0 / math.sqrt(HD)
    doc_ends = jnp.cumsum(doc_lengths)
    block_index = jnp.arange(NBLK, dtype=jnp.int32)
    block_doc = lax.optimization_barrier(jnp.sum((doc_ends[None, :] <= block_index[:, None]).astype(jnp.int32), axis=1))
    token_doc = jnp.concatenate([jnp.full((margin,), -1, jnp.int32), jnp.repeat(block_doc, BLK)])
    keys_pad = jnp.concatenate([jnp.zeros((margin, KVH * HD), key_heads.dtype), key_heads], 0)
    vals_pad = jnp.concatenate([jnp.zeros((margin, KVH * HD), value_heads.dtype), value_heads], 0)
    zero_acc = jnp.zeros((margin + TOKENS, KVH * HD), jnp.float32)

    def step_block(carry, block):
        key_acc, val_acc = carry
        start = (block * BLK).astype(jnp.int32)
        queries = lax.dynamic_slice_in_dim(query_heads, start, BLK, 0).astype(jnp.float32).reshape(BLK, KVH, per_kv, HD)
        grads = lax.dynamic_slice_in_dim(grad_rows, start, BLK, 0).astype(jnp.float32).reshape(BLK, KVH, per_kv, HD)
        keys_win = lax.dynamic_slice_in_dim(keys_pad, start, window, 0).astype(jnp.float32).reshape(window, KVH, HD)
        vals_win = lax.dynamic_slice_in_dim(vals_pad, start, window, 0).astype(jnp.float32).reshape(window, KVH, HD)
        query_doc = lax.dynamic_slice_in_dim(token_doc, start + margin, BLK, 0)
        key_doc = lax.dynamic_slice_in_dim(token_doc, start, window, 0)
        places = jnp.arange(window, dtype=jnp.int32)
        query_places = margin + jnp.arange(BLK, dtype=jnp.int32)
        allowed = (query_doc[:, None] == key_doc[None, :]) & (places[None, :] <= query_places[:, None])
        scores = jnp.einsum('tgqd,kgd->gqtk', queries, keys_win) * scaling
        scores = jnp.where(allowed, scores, -jnp.inf)
        row_max = lax.optimization_barrier(jnp.max(scores, axis=-1, keepdims=True))
        log_norm = row_max + jnp.log(lax.optimization_barrier(jnp.sum(jnp.exp(scores - row_max), axis=-1, keepdims=True)))
        prob_full = jnp.exp(scores - log_norm)
        prob_half = lax.optimization_barrier(prob_full.astype(jnp.bfloat16)).astype(jnp.float32)
        output_half = jnp.einsum('gqtk,kgd->tgqd', prob_half, vals_win).astype(jnp.bfloat16)
        output_back = lax.optimization_barrier(output_half).astype(jnp.float32)
        delta = lax.optimization_barrier(jnp.sum(grads * output_back, axis=-1))
        d_prob = jnp.einsum('tgqd,kgd->gqtk', grads, vals_win)
        d_score = prob_full * (d_prob - jnp.transpose(delta, (1, 2, 0))[..., None])
        d_score_half = lax.optimization_barrier(d_score.astype(jnp.bfloat16)).astype(jnp.float32)
        d_query_blk = (jnp.einsum('gqtk,kgd->tgqd', d_score_half, keys_win) * scaling).astype(jnp.bfloat16)
        d_key_win = jnp.einsum('gqtk,tgqd->kgd', d_score_half, queries) * scaling
        d_val_win = jnp.einsum('gqtk,tgqd->kgd', prob_half, grads)
        old_keys = lax.dynamic_slice_in_dim(key_acc, start, window, 0)
        key_acc = lax.dynamic_update_slice_in_dim(key_acc, old_keys + d_key_win.reshape(window, KVH * HD), start, 0)
        old_vals = lax.dynamic_slice_in_dim(val_acc, start, window, 0)
        val_acc = lax.dynamic_update_slice_in_dim(val_acc, old_vals + d_val_win.reshape(window, KVH * HD), start, 0)
        return ((key_acc, val_acc), (output_half.reshape(BLK, H * HD), d_query_blk.reshape(BLK, H * HD)))
    (key_acc, val_acc), (outputs, d_queries) = lax.scan(step_block, (zero_acc, zero_acc), block_index)
    attn_out = outputs.reshape(TOKENS, H * HD)
    d_query = d_queries.reshape(TOKENS, H * HD)
    d_key = key_acc[margin:].astype(jnp.bfloat16)
    d_value = val_acc[margin:].astype(jnp.bfloat16)
    return (attn_out, d_query, d_key, d_value)
```

```python
import functools
import math

import jax
import jax.numpy as jnp
from jax import lax
from jax.experimental import pallas as pl
from jax.experimental.pallas import tpu as pltpu
from jax.sharding import PartitionSpec as P

H = 32
KVH = 8
HD = 128
BLK = 128
SLOTS = 4
NEG = -1e30
NT = (((1,), (1,)), ((), ()))
F32 = jnp.float32
BF16 = jnp.bfloat16


def kernel(
    dims,
    docs_ref,
    q_ref,
    k_ref,
    v_ref,
    g_ref,
    attn_ref,
    dq_ref,
    dk_ref,
    dv_ref,
    win,
    grads,
    bias,
    outs,
    acc,
    terms,
    arrived,
    fsend,
    final,
    win_send,
    win_recv,
    g_send,
    g_recv,
    o_send,
    o_recv,
    r_send,
    r_recv,
    f_send,
    f_recv,
):
    ctx, tp, groups, per, sharing = dims
    tokens = q_ref.shape[0]
    rows = g_ref.shape[0]
    width = groups * per * HD
    gw = per * HD
    scaling = 1.0 / math.sqrt(HD)
    p = lax.axis_index("ctx")
    t = lax.axis_index("tp")
    even = lax.rem(p, 2) == 0
    odd = jnp.logical_not(even)
    mate = jnp.where(even, p + 1, p - 1)
    low2 = p >= 2
    high2 = p + 2 < ctx
    first_group = t * (groups * per) // (H // KVH)
    my_rows = pl.ds(pl.multiple_of(t * rows, rows), rows)

    def lanes(start, size):
        return pl.ds(pl.multiple_of(start, HD), size)

    barrier = pltpu.get_barrier_semaphore()

    def greet(device):
        pl.semaphore_signal(barrier, inc=1, device_id=device, device_id_type=pl.DeviceIdType.MESH)

    for k in range(1, tp):
        greet({"tp": lax.rem(t + k, tp)})
    greet({"ctx": mate})
    pl.when(low2)(lambda: greet({"ctx": p - 2}))
    pl.when(high2)(lambda: greet({"ctx": p + 2}))
    for j in range(groups):
        cols = lanes((first_group + j) * HD, HD)
        win[j, 0, 0] = k_ref[:, cols]
        win[j, 0, 1] = v_ref[:, cols]
    pl.semaphore_wait(barrier, tp + jnp.where(low2, 1, 0) + jnp.where(high2, 1, 0))

    def remote(src, dst, send, recv, device):
        return pltpu.make_async_remote_copy(
            src_ref=src,
            dst_ref=dst,
            send_sem=send,
            recv_sem=recv,
            device_id=device,
            device_id_type=pl.DeviceIdType.MESH,
        )

    def slab(j, kind, source, slot, device):
        return remote(
            win.at[j, source], win.at[j, slot], win_send.at[j, kind], win_recv.at[j, slot], device
        )

    def grad_copy(j, k):
        peer = lax.rem(t + k, tp)
        return remote(
            g_ref.at[:, lanes(peer * width + j * gw, gw)],
            grads.at[my_rows, pl.ds(j * gw, gw)],
            g_send.at[j, k],
            g_recv.at[j, k],
            {"tp": peer},
        )

    for j in range(groups):
        pl.when(high2)(lambda: slab(j, 0, 0, 2, {"ctx": p + 2}).start())
        pl.when(even)(lambda: slab(j, 1, 0, 1, {"ctx": p + 1}).start())
        for k in range(1, tp):
            grad_copy(j, k).start()

    for d in range(1, SLOTS):

        @pl.when(p < d)
        def _(d=d):
            for j in range(groups):
                win[j, d] = jnp.zeros(win.shape[2:], BF16)

    grads[my_rows, :] = g_ref[:, lanes(t * width, width)]

    for j in range(groups):

        @pl.when(low2)
        def _(j=j):
            slab(j, 0, 0, 2, {"ctx": p - 2}).wait_recv()
            pl.when(even)(lambda: slab(j, 2, 2, 3, {"ctx": p + 1}).start())
            pl.when(odd)(lambda: slab(j, 2, 2, 1, {"ctx": p - 1}).start())

    blocks = tokens // BLK
    ends = []
    total = jnp.int32(0)
    for i in range(docs_ref.shape[0]):
        total = total + docs_ref[i]
        ends.append(total)

    def doc_of(block):
        count = jnp.int32(0)
        for end in ends:
            count = count + jnp.where(end <= block, 1, 0)
        return jnp.where(block >= 0, count, -1)

    causal = lax.broadcasted_iota(jnp.int32, (BLK, BLK), 0) <= lax.broadcasted_iota(
        jnp.int32, (BLK, BLK), 1
    )
    query_docs = [doc_of(p * blocks + b) for b in range(blocks)]
    for d in range(SLOTS):
        for kb in range(blocks):
            key_doc = query_docs[kb] if d == 0 else doc_of((p - d) * blocks + kb)
            for qb in range(blocks):
                if d == 0 and kb > qb:
                    tile = jnp.full((BLK, BLK), NEG, F32)
                elif d == 0 and kb == qb:
                    tile = jnp.where(causal, 0.0, NEG).astype(F32)
                else:
                    level = jnp.where(key_doc == query_docs[qb], 0.0, NEG).astype(F32)
                    tile = jnp.full((BLK, BLK), level, F32)
                bias[pl.ds(d * tokens + kb * BLK, BLK), pl.ds(qb * BLK, BLK)] = tile

    for j in range(groups):
        pl.when(p >= 1)(lambda: slab(j, 0, 0, 1, {"ctx": mate}).wait_recv())
        pl.when(even & low2 & high2)(lambda: slab(j, 3, 1, 3, {"ctx": p + 2}).start())

    span = SLOTS * tokens

    def head(j, i, keys, vals, keys_t, vals_t):
        cols = lanes((j * per + i) * HD, HD)
        queries = q_ref[:, cols]
        grad = grads[:, cols]
        scores = lax.dot_general(keys, queries, NT, preferred_element_type=F32)
        scores = scores * scaling + bias[...]
        e = jnp.exp(scores - jnp.max(scores, axis=0, keepdims=True))
        prob = e * (1.0 / jnp.sum(e, axis=0, keepdims=True))
        half = prob.astype(BF16)
        out_t = jnp.dot(vals_t, half, preferred_element_type=F32).astype(BF16).astype(F32)
        outs[:, cols] = out_t.T.astype(BF16)
        delta = jnp.sum(grad.astype(F32).T * out_t, axis=0, keepdims=True)
        d_prob = lax.dot_general(vals, grad, NT, preferred_element_type=F32)
        d_score = (prob * (d_prob - delta)).astype(BF16)
        dq_t = jnp.dot(keys_t, d_score, preferred_element_type=F32) * scaling
        dq_ref[:, cols] = dq_t.T.astype(BF16)
        d_key = jnp.dot(d_score, queries, preferred_element_type=F32) * scaling
        d_val = jnp.dot(half, grad, preferred_element_type=F32)
        acc[j, :, 0] += d_key.reshape(SLOTS, tokens, HD)
        acc[j, :, 1] += d_val.reshape(SLOTS, tokens, HD)

    def term(j, kind, place, device):
        return remote(
            terms.at[j, kind], arrived.at[j, place], r_send.at[j, kind], r_recv.at[j, place], device
        )

    def out_copy(j, k):
        peer = lax.rem(t + k, tp)
        return remote(
            outs.at[pl.ds(pl.multiple_of(peer * rows, rows), rows), pl.ds(j * gw, gw)],
            attn_ref.at[:, lanes(t * width + j * gw, gw)],
            o_send.at[j, k],
            o_recv.at[j, k],
            {"tp": peer},
        )

    def fin_copy(j, k):
        peer = lax.rem(t + k, tp)
        return remote(
            fsend.at[j, :, pl.ds(pl.multiple_of(peer * rows, rows), rows)],
            final.at[t, j],
            f_send.at[j, k],
            f_recv.at[j, k],
            {"tp": peer},
        )

    def step_a(j):
        @pl.when(p >= 3)
        def _():
            terms[j, 3] = acc[j, 3].astype(BF16)
            pl.when(even)(lambda: term(j, 3, 0, {"ctx": p - 2}).start())
            pl.when(odd)(lambda: term(j, 3, 1, {"ctx": p - 1}).start())

        @pl.when(odd)
        def _():
            terms[j, 1] = acc[j, 1].astype(BF16)
            term(j, 1, 2, {"ctx": p - 1}).start()

    def step_b(j):
        @pl.when(even & low2)
        def _():
            @pl.when(high2)
            def _():
                term(j, 3, 0, {"ctx": p + 2}).wait_recv()
                acc[j, 1] += arrived[j, 0].astype(F32)

            terms[j, 1] = acc[j, 1].astype(BF16)
            term(j, 1, 1, {"ctx": p + 1}).start()

    def step_c(j):
        @pl.when(low2)
        def _():
            term(j, 3, 1, {"ctx": mate}).wait_recv()
            terms[j, 2] = (acc[j, 2] + arrived[j, 1].astype(F32)).astype(BF16)
            term(j, 2, 3, {"ctx": p - 2}).start()

    def step_d(j):
        @pl.when(even)
        def _():
            term(j, 1, 2, {"ctx": p + 1}).wait_recv()
            acc[j, 0] += arrived[j, 2].astype(F32)

        @pl.when(high2)
        def _():
            term(j, 2, 3, {"ctx": p + 2}).wait_recv()
            acc[j, 0] += arrived[j, 3].astype(F32)

        fsend[j] = acc[j, 0].astype(fsend.dtype)
        for k in range(1, tp):
            fin_copy(j, k).start()
        final[t, j] = fsend[j, :, my_rows]

    acc[...] = jnp.zeros(acc.shape, F32)
    pending = []
    for j in range(groups):
        for k in range(1, tp):
            grad_copy(j, k).wait_recv()
        pl.when(low2 & (p >= 3))(lambda: slab(j, 2, 2, 3, {"ctx": mate}).wait_recv())
        keys = win[j, :, 0].reshape(span, HD)
        vals = win[j, :, 1].reshape(span, HD)
        keys_t = keys.astype(F32).T.astype(BF16)
        vals_t = vals.astype(F32).T.astype(BF16)
        if j == 0 and groups > 1:

            @pl.loop(0, per)
            def _(i):
                head(j, i, keys, vals, keys_t, vals_t)
        else:
            for i in range(per):
                head(j, i, keys, vals, keys_t, vals_t)
                if pending:
                    pending.pop(0)()
        for step in pending:
            step()
        step_a(j)
        pending = [functools.partial(f, j) for f in (step_b, step_c, step_d)]
        for k in range(1, tp):
            out_copy(j, k).start()
        cols = lanes(t * width + j * gw, gw)
        attn_ref[:, cols] = outs[my_rows, pl.ds(j * gw, gw)]
    for step in pending:
        step()

    for j in range(groups):
        for k in range(1, tp):
            fin_copy(j, k).wait_recv()
            out_copy(j, k).wait_recv()
    for head_group in range(KVH):
        owner, j = head_group * sharing // groups, head_group % groups
        both = final[owner, j].astype(F32)
        for s in range(1, sharing):
            both = both + final[owner + s, j].astype(F32)
        cols = pl.ds(head_group * HD, HD)
        dk_ref[:, cols] = both[0].astype(BF16)
        dv_ref[:, cols] = both[1].astype(BF16)

    for j in range(groups):
        for k in range(1, tp):
            grad_copy(j, k).wait_send()
            out_copy(j, k).wait_send()
            fin_copy(j, k).wait_send()
        pl.when(high2)(lambda: slab(j, 0, 0, 2, {"ctx": p + 2}).wait_send())
        pl.when(even)(lambda: slab(j, 1, 0, 1, {"ctx": p + 1}).wait_send())
        pl.when(low2)(lambda: slab(j, 2, 2, 3, {"ctx": mate}).wait_send())
        pl.when(even & low2 & high2)(lambda: slab(j, 3, 1, 3, {"ctx": p + 2}).wait_send())
        pl.when(p >= 3)(lambda: term(j, 3, 0, {"ctx": mate}).wait_send())
        pl.when(p >= 1)(lambda: term(j, 1, 2, {"ctx": mate}).wait_send())
        pl.when(low2)(lambda: term(j, 2, 3, {"ctx": p - 2}).wait_send())


def local(ctx, tp, query_heads, key_heads, value_heads, grad_rows, doc_lengths):
    tokens, width = query_heads.shape
    rows = grad_rows.shape[0]
    heads_dev = width // HD
    per_kv = H // KVH
    groups = max(1, heads_dev // per_kv)
    sharing = max(1, per_kv // heads_dev)
    per = heads_dev // groups
    final_type = BF16 if sharing == 1 else F32
    vmem = pl.BlockSpec(memory_space=pltpu.VMEM)
    dma = pltpu.SemaphoreType.DMA
    pair = (2, tokens, HD)
    return pl.pallas_call(
        functools.partial(kernel, (ctx, tp, groups, per, sharing)),
        out_shape=(
            jax.ShapeDtypeStruct((rows, H * HD), BF16),
            jax.ShapeDtypeStruct((tokens, width), BF16),
            jax.ShapeDtypeStruct((rows, KVH * HD), BF16),
            jax.ShapeDtypeStruct((rows, KVH * HD), BF16),
        ),
        in_specs=[pl.BlockSpec(memory_space=pltpu.SMEM)] + [vmem] * 4,
        out_specs=(vmem,) * 4,
        scratch_shapes=[
            pltpu.VMEM((groups, SLOTS) + pair, BF16),
            pltpu.VMEM((tokens, width), BF16),
            pltpu.VMEM((SLOTS * tokens, tokens), F32),
            pltpu.VMEM((tokens, width), BF16),
            pltpu.VMEM((groups, SLOTS) + pair, F32),
            pltpu.VMEM((groups, SLOTS) + pair, BF16),
            pltpu.VMEM((groups, SLOTS) + pair, BF16),
            pltpu.VMEM((groups,) + pair, final_type),
            pltpu.VMEM((tp, groups, 2, rows, HD), final_type),
            dma((groups, 4)),
            dma((groups, SLOTS)),
            dma((groups, tp)),
            dma((groups, tp)),
            dma((groups, tp)),
            dma((groups, tp)),
            dma((groups, SLOTS)),
            dma((groups, SLOTS)),
            dma((groups, tp)),
            dma((groups, tp)),
        ],
        compiler_params=pltpu.CompilerParams(
            collective_id=0, has_side_effects=True, vmem_limit_bytes=48 * 1024 * 1024
        ),
    )(doc_lengths, query_heads, key_heads, value_heads, grad_rows)


def solution(mesh):
    return jax.shard_map(
        functools.partial(local, mesh.shape["ctx"], mesh.shape["tp"]),
        mesh=mesh,
        in_specs=(P("ctx", "tp"), P("ctx", None), P("ctx", None), P(("ctx", "tp"), None), P()),
        out_specs=(
            P(("ctx", "tp"), None),
            P("ctx", "tp"),
            P(("ctx", "tp"), None),
            P(("ctx", "tp"), None),
        ),
        check_vma=False,
    )
```

```python
import functools
import math

import jax
import jax.numpy as jnp
from jax import lax
from jax.experimental import pallas as pl
from jax.experimental.pallas import tpu as pltpu
from jax.sharding import PartitionSpec as P

H = 32
KVH = 8
HD = 128
BLK = 128
SLOTS = 4
NEG = -1e30
NT = (((1,), (1,)), ((), ()))
F32 = jnp.float32
BF16 = jnp.bfloat16


def kernel(
    dims,
    docs_ref,
    q_ref,
    k_ref,
    v_ref,
    g_ref,
    attn_ref,
    dq_ref,
    dk_ref,
    dv_ref,
    win,
    grads,
    q_all,
    g_all,
    bias,
    probs,
    dq_sum,
    outs,
    acc,
    terms,
    arrived,
    fsend,
    final,
    win_send,
    win_recv,
    g_send,
    g_recv,
    o_send,
    o_recv,
    r_send,
    r_recv,
    f_send,
    f_recv,
    in_sem,
):
    ctx, tp, groups, per, sharing = dims
    tokens = q_ref.shape[0]
    rows = g_ref.shape[0]
    width = groups * per * HD
    gw = per * HD
    scaling = 1.0 / math.sqrt(HD)
    p = lax.axis_index("ctx")
    t = lax.axis_index("tp")
    even = lax.rem(p, 2) == 0
    odd = jnp.logical_not(even)
    mate = jnp.where(even, p + 1, p - 1)
    low2 = p >= 2
    high2 = p + 2 < ctx
    first_group = t * (groups * per) // (H // KVH)
    my_rows = pl.ds(pl.multiple_of(t * rows, rows), rows)

    def lanes(start, size):
        return pl.ds(pl.multiple_of(start, HD), size)

    barrier = pltpu.get_barrier_semaphore()

    def greet(device):
        pl.semaphore_signal(barrier, inc=1, device_id=device, device_id_type=pl.DeviceIdType.MESH)

    for k in range(1, tp):
        greet({"tp": lax.rem(t + k, tp)})
    greet({"ctx": mate})
    pl.when(low2)(lambda: greet({"ctx": p - 2}))
    pl.when(high2)(lambda: greet({"ctx": p + 2}))
    loads = []

    def load(src, dst):
        copy = pltpu.make_async_copy(src, dst, in_sem.at[len(loads)])
        copy.start()
        loads.append(copy)

    for j in range(groups):
        cols = lanes((first_group + j) * HD, HD)
        load(k_ref.at[:, cols], win.at[j, 0, 0])
        load(v_ref.at[:, cols], win.at[j, 0, 1])
    load(g_ref.at[:, lanes(t * width, width)], grads.at[my_rows])
    for j in range(groups):
        for i in range(per):
            load(
                q_ref.at[:, pl.ds((j * per + i) * HD, HD)],
                q_all.at[j, pl.ds(i * tokens, tokens)],
            )
    for copy in loads[: 2 * groups]:
        copy.wait()
    pl.semaphore_wait(barrier, tp + jnp.where(low2, 1, 0) + jnp.where(high2, 1, 0))

    def remote(src, dst, send, recv, device):
        return pltpu.make_async_remote_copy(
            src_ref=src,
            dst_ref=dst,
            send_sem=send,
            recv_sem=recv,
            device_id=device,
            device_id_type=pl.DeviceIdType.MESH,
        )

    def slab(j, kind, source, slot, device):
        return remote(
            win.at[j, source], win.at[j, slot], win_send.at[j, kind], win_recv.at[j, slot], device
        )

    def grad_copy(j, k):
        peer = lax.rem(t + k, tp)
        return remote(
            g_ref.at[:, lanes(peer * width + j * gw, gw)],
            grads.at[my_rows, pl.ds(j * gw, gw)],
            g_send.at[j, k],
            g_recv.at[j, k],
            {"tp": peer},
        )

    for j in range(groups):
        pl.when(high2)(lambda: slab(j, 0, 0, 2, {"ctx": p + 2}).start())
        pl.when(even)(lambda: slab(j, 1, 0, 1, {"ctx": p + 1}).start())
        for k in range(1, tp):
            grad_copy(j, k).start()

    for d in range(1, SLOTS):

        @pl.when(p < d)
        def _(d=d):
            for j in range(groups):
                win[j, d] = jnp.zeros(win.shape[2:], BF16)

    blocks = tokens // BLK
    ends = []
    total = jnp.int32(0)
    for i in range(docs_ref.shape[0]):
        total = total + docs_ref[i]
        ends.append(total)

    def doc_of(block):
        count = jnp.int32(0)
        for end in ends:
            count = count + jnp.where(end <= block, 1, 0)
        return jnp.where(block >= 0, count, -1)

    causal = lax.broadcasted_iota(jnp.int32, (BLK, BLK), 0) <= lax.broadcasted_iota(
        jnp.int32, (BLK, BLK), 1
    )
    query_docs = [doc_of(p * blocks + b) for b in range(blocks)]
    for d in range(SLOTS):
        for kb in range(blocks):
            key_doc = query_docs[kb] if d == 0 else doc_of((p - d) * blocks + kb)
            for qb in range(blocks):
                if d == 0 and kb > qb:
                    tile = jnp.full((BLK, BLK), NEG, F32)
                elif d == 0 and kb == qb:
                    tile = jnp.where(causal, 0.0, NEG).astype(F32)
                else:
                    level = jnp.where(key_doc == query_docs[qb], 0.0, NEG).astype(F32)
                    tile = jnp.full((BLK, BLK), level, F32)
                bias[pl.ds(d * tokens + kb * BLK, BLK), pl.ds(qb * BLK, BLK)] = tile

    for copy in loads[2 * groups :]:
        copy.wait()

    def scores(j, d):
        wide = lax.dot_general(win[j, d, 0], q_all[j], NT, preferred_element_type=F32)
        tile = bias[pl.ds(d * tokens, tokens), :]
        probs[j, d] = wide * scaling + jnp.concatenate([tile] * per, axis=1)

    for j in range(groups):

        @pl.when(low2)
        def _(j=j):
            slab(j, 0, 0, 2, {"ctx": p - 2}).wait_recv()
            pl.when(even)(lambda: slab(j, 2, 2, 3, {"ctx": p + 1}).start())
            pl.when(odd)(lambda: slab(j, 2, 2, 1, {"ctx": p - 1}).start())

    for j in range(groups):
        scores(j, 0)
    for j in range(groups):
        pl.when(p >= 1)(lambda: slab(j, 0, 0, 1, {"ctx": mate}).wait_recv())
        pl.when(even & low2 & high2)(lambda: slab(j, 3, 1, 3, {"ctx": p + 2}).start())

    for j in range(groups):
        scores(j, 2)
    for j in range(groups):
        scores(j, 1)

    def across(value):
        return value.astype(F32).T

    def forward(j):
        top = jnp.max(probs[j, 0], axis=0, keepdims=True)
        for d in range(1, SLOTS):
            top = jnp.maximum(top, jnp.max(probs[j, d], axis=0, keepdims=True))
        norm = jnp.zeros_like(top)
        for d in range(SLOTS):
            e = jnp.exp(probs[j, d] - top)
            probs[j, d] = e
            norm = norm + jnp.sum(e, axis=0, keepdims=True)
        inverse = 1.0 / norm
        out_t = jnp.zeros((HD, per * tokens), F32)
        for d in range(SLOTS):
            prob = probs[j, d] * inverse
            probs[j, d] = prob
            vals_t = across(win[j, d, 1]).astype(BF16)
            out_t = out_t + jnp.dot(vals_t, prob.astype(BF16), preferred_element_type=F32)
        out_t = out_t.astype(BF16).astype(F32)
        rows_of = out_t.T.astype(BF16)
        for i in range(per):
            cols = pl.ds((j * per + i) * HD, HD)
            outs[:, cols] = rows_of[i * tokens : (i + 1) * tokens]
        return out_t

    def delta_of(j, out_t):
        for i in range(per):
            cols = pl.ds((j * per + i) * HD, HD)
            g_all[j, pl.ds(i * tokens, tokens)] = grads[:, cols]
        return jnp.sum(across(g_all[j]) * out_t, axis=0, keepdims=True)

    def backward(j, d, delta, first):
        d_prob = lax.dot_general(win[j, d, 1], g_all[j], NT, preferred_element_type=F32)
        prob = probs[j, d]
        d_score = (prob * (d_prob - delta)).astype(BF16)
        keys_t = across(win[j, d, 0]).astype(BF16)
        dq_t = jnp.dot(keys_t, d_score, preferred_element_type=F32)
        dq_sum[j] = dq_t if first else dq_sum[j] + dq_t
        acc[j, d, 0] = jnp.dot(d_score, q_all[j], preferred_element_type=F32) * scaling
        acc[j, d, 1] = jnp.dot(prob.astype(BF16), g_all[j], preferred_element_type=F32)

    def finish_query(j):
        rows_of = (dq_sum[j] * scaling).T.astype(BF16)
        for i in range(per):
            cols = pl.ds((j * per + i) * HD, HD)
            dq_ref[:, cols] = rows_of[i * tokens : (i + 1) * tokens]

    def term(j, kind, place, device):
        return remote(
            terms.at[j, kind], arrived.at[j, place], r_send.at[j, kind], r_recv.at[j, place], device
        )

    def out_copy(j, k):
        peer = lax.rem(t + k, tp)
        return remote(
            outs.at[pl.ds(pl.multiple_of(peer * rows, rows), rows), pl.ds(j * gw, gw)],
            attn_ref.at[:, lanes(t * width + j * gw, gw)],
            o_send.at[j, k],
            o_recv.at[j, k],
            {"tp": peer},
        )

    def fin_copy(j, k):
        peer = lax.rem(t + k, tp)
        return remote(
            fsend.at[j, :, pl.ds(pl.multiple_of(peer * rows, rows), rows)],
            final.at[t, j],
            f_send.at[j, k],
            f_recv.at[j, k],
            {"tp": peer},
        )

    def step_a3(j):
        @pl.when(p >= 3)
        def _():
            terms[j, 3] = acc[j, 3].astype(BF16)
            pl.when(even)(lambda: term(j, 3, 0, {"ctx": p - 2}).start())
            pl.when(odd)(lambda: term(j, 3, 1, {"ctx": p - 1}).start())

    def step_a1(j):
        @pl.when(odd)
        def _():
            terms[j, 1] = acc[j, 1].astype(BF16)
            term(j, 1, 2, {"ctx": p - 1}).start()

    def step_b(j):
        @pl.when(even & low2)
        def _():
            @pl.when(high2)
            def _():
                term(j, 3, 0, {"ctx": p + 2}).wait_recv()
                acc[j, 1] += arrived[j, 0].astype(F32)

            terms[j, 1] = acc[j, 1].astype(BF16)
            term(j, 1, 1, {"ctx": p + 1}).start()

    def step_c(j):
        @pl.when(low2)
        def _():
            term(j, 3, 1, {"ctx": mate}).wait_recv()
            terms[j, 2] = (acc[j, 2] + arrived[j, 1].astype(F32)).astype(BF16)
            term(j, 2, 3, {"ctx": p - 2}).start()

    def step_d(j):
        @pl.when(even)
        def _():
            term(j, 1, 2, {"ctx": p + 1}).wait_recv()
            acc[j, 0] += arrived[j, 2].astype(F32)

        @pl.when(high2)
        def _():
            term(j, 2, 3, {"ctx": p + 2}).wait_recv()
            acc[j, 0] += arrived[j, 3].astype(F32)

        fsend[j] = acc[j, 0].astype(fsend.dtype)
        for k in range(1, tp):
            fin_copy(j, k).start()
        final[t, j] = fsend[j, :, my_rows]

    deltas = []
    for j in range(groups):
        pl.when(p >= 3)(lambda: slab(j, 2, 2, 3, {"ctx": mate}).wait_recv())
        scores(j, 3)
        out_t = forward(j)
        for k in range(1, tp):
            out_copy(j, k).start()
        cols = lanes(t * width + j * gw, gw)
        attn_ref[:, cols] = outs[my_rows, pl.ds(j * gw, gw)]
        for k in range(1, tp):
            grad_copy(j, k).wait_recv()
        deltas.append(delta_of(j, out_t))
    for j in range(groups):
        backward(j, 3, deltas[j], True)
        step_a3(j)
    for j in range(groups):
        backward(j, 1, deltas[j], False)
        step_a1(j)
    for j in range(groups):
        step_b(j)
        backward(j, 2, deltas[j], False)
    for j in range(groups):
        backward(j, 0, deltas[j], False)
        step_c(j)
    for j in range(groups):
        finish_query(j)
    for j in range(groups):
        step_d(j)

    for j in range(groups):
        for k in range(1, tp):
            fin_copy(j, k).wait_recv()
            out_copy(j, k).wait_recv()
    for head_group in range(KVH):
        owner, j = head_group * sharing // groups, head_group % groups
        both = final[owner, j].astype(F32)
        for s in range(1, sharing):
            both = both + final[owner + s, j].astype(F32)
        cols = pl.ds(head_group * HD, HD)
        dk_ref[:, cols] = both[0].astype(BF16)
        dv_ref[:, cols] = both[1].astype(BF16)

    for j in range(groups):
        for k in range(1, tp):
            grad_copy(j, k).wait_send()
            out_copy(j, k).wait_send()
            fin_copy(j, k).wait_send()
        pl.when(high2)(lambda: slab(j, 0, 0, 2, {"ctx": p + 2}).wait_send())
        pl.when(even)(lambda: slab(j, 1, 0, 1, {"ctx": p + 1}).wait_send())
        pl.when(low2)(lambda: slab(j, 2, 2, 3, {"ctx": mate}).wait_send())
        pl.when(even & low2 & high2)(lambda: slab(j, 3, 1, 3, {"ctx": p + 2}).wait_send())
        pl.when(p >= 3)(lambda: term(j, 3, 0, {"ctx": mate}).wait_send())
        pl.when(p >= 1)(lambda: term(j, 1, 2, {"ctx": mate}).wait_send())
        pl.when(low2)(lambda: term(j, 2, 3, {"ctx": p - 2}).wait_send())


def local(ctx, tp, query_heads, key_heads, value_heads, grad_rows, doc_lengths):
    tokens, width = query_heads.shape
    rows = grad_rows.shape[0]
    heads_dev = width // HD
    per_kv = H // KVH
    groups = max(1, heads_dev // per_kv)
    sharing = max(1, per_kv // heads_dev)
    per = heads_dev // groups
    final_type = BF16 if sharing == 1 else F32
    vmem = pl.BlockSpec(memory_space=pltpu.VMEM)
    dma = pltpu.SemaphoreType.DMA
    pair = (2, tokens, HD)
    return pl.pallas_call(
        functools.partial(kernel, (ctx, tp, groups, per, sharing)),
        out_shape=(
            jax.ShapeDtypeStruct((rows, H * HD), BF16),
            jax.ShapeDtypeStruct((tokens, width), BF16),
            jax.ShapeDtypeStruct((rows, KVH * HD), BF16),
            jax.ShapeDtypeStruct((rows, KVH * HD), BF16),
        ),
        in_specs=[pl.BlockSpec(memory_space=pltpu.SMEM)] + [pl.BlockSpec(memory_space=pltpu.HBM)] * 4,
        out_specs=(vmem,) * 4,
        scratch_shapes=[
            pltpu.VMEM((groups, SLOTS) + pair, BF16),
            pltpu.VMEM((tokens, width), BF16),
            pltpu.VMEM((groups, per * tokens, HD), BF16),
            pltpu.VMEM((groups, per * tokens, HD), BF16),
            pltpu.VMEM((SLOTS * tokens, tokens), F32),
            pltpu.VMEM((groups, SLOTS, tokens, per * tokens), F32),
            pltpu.VMEM((groups, HD, per * tokens), F32),
            pltpu.VMEM((tokens, width), BF16),
            pltpu.VMEM((groups, SLOTS) + pair, F32),
            pltpu.VMEM((groups, SLOTS) + pair, BF16),
            pltpu.VMEM((groups, SLOTS) + pair, BF16),
            pltpu.VMEM((groups,) + pair, final_type),
            pltpu.VMEM((tp, groups, 2, rows, HD), final_type),
            dma((groups, 4)),
            dma((groups, SLOTS)),
            dma((groups, tp)),
            dma((groups, tp)),
            dma((groups, tp)),
            dma((groups, tp)),
            dma((groups, SLOTS)),
            dma((groups, SLOTS)),
            dma((groups, tp)),
            dma((groups, tp)),
            dma((2 * groups + 1 + groups * per,)),
        ],
        compiler_params=pltpu.CompilerParams(
            collective_id=0, has_side_effects=True, vmem_limit_bytes=62 * 1024 * 1024
        ),
    )(doc_lengths, query_heads, key_heads, value_heads, grad_rows)


def solution(mesh):
    return jax.shard_map(
        functools.partial(local, mesh.shape["ctx"], mesh.shape["tp"]),
        mesh=mesh,
        in_specs=(P("ctx", "tp"), P("ctx", None), P("ctx", None), P(("ctx", "tp"), None), P()),
        out_specs=(
            P(("ctx", "tp"), None),
            P("ctx", "tp"),
            P(("ctx", "tp"), None),
            P(("ctx", "tp"), None),
        ),
        check_vma=False,
    )
```

```python
import functools
import math

import jax
import jax.numpy as jnp
from jax import lax
from jax.experimental import pallas as pl
from jax.experimental.pallas import tpu as pltpu
from jax.sharding import PartitionSpec as P

H = 32
KVH = 8
HD = 128
BLK = 128
SLOTS = 4
NEG = -1e30
NT = (((1,), (1,)), ((), ()))
F32 = jnp.float32
BF16 = jnp.bfloat16


def kernel(
    dims,
    docs_ref,
    q_ref,
    k_ref,
    v_ref,
    g_ref,
    attn_ref,
    dq_ref,
    dk_ref,
    dv_ref,
    win,
    grads,
    q_all,
    g_all,
    bias,
    probs,
    dq_sum,
    outs,
    acc,
    terms,
    arrived,
    fsend,
    final,
    win_send,
    win_recv,
    g_send,
    g_recv,
    o_send,
    o_recv,
    r_send,
    r_recv,
    f_send,
    f_recv,
    in_sem,
    dq_held,
    kv_held,
    out_sem,
):
    ctx, tp, groups, per, sharing = dims
    tokens = q_ref.shape[0]
    rows = g_ref.shape[0]
    width = groups * per * HD
    gw = per * HD
    scaling = 1.0 / math.sqrt(HD)
    p = lax.axis_index("ctx")
    t = lax.axis_index("tp")
    even = lax.rem(p, 2) == 0
    odd = jnp.logical_not(even)
    mate = jnp.where(even, p + 1, p - 1)
    low2 = p >= 2
    high2 = p + 2 < ctx
    first_group = t * (groups * per) // (H // KVH)
    my_rows = pl.ds(pl.multiple_of(t * rows, rows), rows)

    def lanes(start, size):
        return pl.ds(pl.multiple_of(start, HD), size)

    barrier = pltpu.get_barrier_semaphore()

    def greet(device):
        pl.semaphore_signal(barrier, inc=1, device_id=device, device_id_type=pl.DeviceIdType.MESH)

    for k in range(1, tp):
        greet({"tp": lax.rem(t + k, tp)})
    greet({"ctx": mate})
    pl.when(low2)(lambda: greet({"ctx": p - 2}))
    pl.when(high2)(lambda: greet({"ctx": p + 2}))
    loads = []

    def load(src, dst):
        copy = pltpu.make_async_copy(src, dst, in_sem.at[len(loads)])
        copy.start()
        loads.append(copy)

    for j in range(groups):
        cols = lanes((first_group + j) * HD, HD)
        load(k_ref.at[:, cols], win.at[j, 0, 0])
        load(v_ref.at[:, cols], win.at[j, 0, 1])
    load(g_ref.at[:, lanes(t * width, width)], grads.at[my_rows])
    for j in range(groups):
        for i in range(per):
            load(
                q_ref.at[:, pl.ds((j * per + i) * HD, HD)],
                q_all.at[j, pl.ds(i * tokens, tokens)],
            )
    for copy in loads[: 2 * groups]:
        copy.wait()
    pl.semaphore_wait(barrier, tp + jnp.where(low2, 1, 0) + jnp.where(high2, 1, 0))

    def remote(src, dst, send, recv, device):
        return pltpu.make_async_remote_copy(
            src_ref=src,
            dst_ref=dst,
            send_sem=send,
            recv_sem=recv,
            device_id=device,
            device_id_type=pl.DeviceIdType.MESH,
        )

    def slab(j, kind, source, slot, device):
        return remote(
            win.at[j, source], win.at[j, slot], win_send.at[j, kind], win_recv.at[j, slot], device
        )

    def grad_copy(j, k):
        peer = lax.rem(t + k, tp)
        return remote(
            g_ref.at[:, lanes(peer * width + j * gw, gw)],
            grads.at[my_rows, pl.ds(j * gw, gw)],
            g_send.at[j, k],
            g_recv.at[j, k],
            {"tp": peer},
        )

    for j in range(groups):
        pl.when(high2)(lambda: slab(j, 0, 0, 2, {"ctx": p + 2}).start())
        pl.when(even)(lambda: slab(j, 1, 0, 1, {"ctx": p + 1}).start())
        for k in range(1, tp):
            grad_copy(j, k).start()

    for d in range(1, SLOTS):

        @pl.when(p < d)
        def _(d=d):
            for j in range(groups):
                win[j, d] = jnp.zeros(win.shape[2:], BF16)

    blocks = tokens // BLK
    ends = []
    total = jnp.int32(0)
    for i in range(docs_ref.shape[0]):
        total = total + docs_ref[i]
        ends.append(total)

    def doc_of(block):
        count = jnp.int32(0)
        for end in ends:
            count = count + jnp.where(end <= block, 1, 0)
        return jnp.where(block >= 0, count, -1)

    causal = lax.broadcasted_iota(jnp.int32, (BLK, BLK), 0) <= lax.broadcasted_iota(
        jnp.int32, (BLK, BLK), 1
    )
    query_docs = [doc_of(p * blocks + b) for b in range(blocks)]
    for d in range(SLOTS):
        for kb in range(blocks):
            key_doc = query_docs[kb] if d == 0 else doc_of((p - d) * blocks + kb)
            for qb in range(blocks):
                if d == 0 and kb > qb:
                    tile = jnp.full((BLK, BLK), NEG, F32)
                elif d == 0 and kb == qb:
                    tile = jnp.where(causal, 0.0, NEG).astype(F32)
                else:
                    level = jnp.where(key_doc == query_docs[qb], 0.0, NEG).astype(F32)
                    tile = jnp.full((BLK, BLK), level, F32)
                bias[pl.ds(d * tokens + kb * BLK, BLK), pl.ds(qb * BLK, BLK)] = tile

    for copy in loads[2 * groups :]:
        copy.wait()

    def scores(j, d):
        wide = lax.dot_general(win[j, d, 0], q_all[j], NT, preferred_element_type=F32)
        tile = bias[pl.ds(d * tokens, tokens), :]
        probs[j, d] = wide * scaling + jnp.concatenate([tile] * per, axis=1)

    for j in range(groups):

        @pl.when(low2)
        def _(j=j):
            slab(j, 0, 0, 2, {"ctx": p - 2}).wait_recv()
            pl.when(even)(lambda: slab(j, 2, 2, 3, {"ctx": p + 1}).start())
            pl.when(odd)(lambda: slab(j, 2, 2, 1, {"ctx": p - 1}).start())

    for j in range(groups):
        scores(j, 0)
    for j in range(groups):
        pl.when(p >= 1)(lambda: slab(j, 0, 0, 1, {"ctx": mate}).wait_recv())
        pl.when(even & low2 & high2)(lambda: slab(j, 3, 1, 3, {"ctx": p + 2}).start())

    for j in range(groups):
        scores(j, 2)
    for j in range(groups):
        scores(j, 1)

    def across(value):
        return value.astype(F32).T

    def forward(j):
        top = jnp.max(probs[j, 0], axis=0, keepdims=True)
        for d in range(1, SLOTS):
            top = jnp.maximum(top, jnp.max(probs[j, d], axis=0, keepdims=True))
        norm = jnp.zeros_like(top)
        for d in range(SLOTS):
            e = jnp.exp(probs[j, d] - top)
            probs[j, d] = e
            norm = norm + jnp.sum(e, axis=0, keepdims=True)
        inverse = 1.0 / norm
        out_t = jnp.zeros((HD, per * tokens), F32)
        for d in range(SLOTS):
            prob = probs[j, d] * inverse
            probs[j, d] = prob
            vals_t = across(win[j, d, 1]).astype(BF16)
            out_t = out_t + jnp.dot(vals_t, prob.astype(BF16), preferred_element_type=F32)
        out_t = out_t.astype(BF16).astype(F32)
        rows_of = out_t.T.astype(BF16)
        for i in range(per):
            cols = pl.ds((j * per + i) * HD, HD)
            outs[:, cols] = rows_of[i * tokens : (i + 1) * tokens]
        return out_t

    def delta_of(j, out_t):
        for i in range(per):
            cols = pl.ds((j * per + i) * HD, HD)
            g_all[j, pl.ds(i * tokens, tokens)] = grads[:, cols]
        return jnp.sum(across(g_all[j]) * out_t, axis=0, keepdims=True)

    def backward(j, d, delta, first):
        d_prob = lax.dot_general(win[j, d, 1], g_all[j], NT, preferred_element_type=F32)
        prob = probs[j, d]
        d_score = (prob * (d_prob - delta)).astype(BF16)
        keys_t = across(win[j, d, 0]).astype(BF16)
        dq_t = jnp.dot(keys_t, d_score, preferred_element_type=F32)
        dq_sum[j] = dq_t if first else dq_sum[j] + dq_t
        acc[j, d, 0] = jnp.dot(d_score, q_all[j], preferred_element_type=F32) * scaling
        acc[j, d, 1] = jnp.dot(prob.astype(BF16), g_all[j], preferred_element_type=F32)

    def finish_query(j):
        rows_of = (dq_sum[j] * scaling).T.astype(BF16)
        for i in range(per):
            cols = pl.ds((j * per + i) * HD, HD)
            dq_held[:, cols] = rows_of[i * tokens : (i + 1) * tokens]
        cols = pl.ds(j * gw, gw)
        store(dq_held.at[:, cols], dq_ref.at[:, cols])

    def term(j, kind, place, device):
        return remote(
            terms.at[j, kind], arrived.at[j, place], r_send.at[j, kind], r_recv.at[j, place], device
        )

    def out_copy(j, k):
        peer = lax.rem(t + k, tp)
        return remote(
            outs.at[pl.ds(pl.multiple_of(peer * rows, rows), rows), pl.ds(j * gw, gw)],
            attn_ref.at[:, lanes(t * width + j * gw, gw)],
            o_send.at[j, k],
            o_recv.at[j, k],
            {"tp": peer},
        )

    def fin_copy(j, k):
        peer = lax.rem(t + k, tp)
        return remote(
            fsend.at[j, :, pl.ds(pl.multiple_of(peer * rows, rows), rows)],
            final.at[t, j],
            f_send.at[j, k],
            f_recv.at[j, k],
            {"tp": peer},
        )

    def step_a3(j):
        @pl.when(p >= 3)
        def _():
            terms[j, 3] = acc[j, 3].astype(BF16)
            pl.when(even)(lambda: term(j, 3, 0, {"ctx": p - 2}).start())
            pl.when(odd)(lambda: term(j, 3, 1, {"ctx": p - 1}).start())

    def step_a1(j):
        @pl.when(odd)
        def _():
            terms[j, 1] = acc[j, 1].astype(BF16)
            term(j, 1, 2, {"ctx": p - 1}).start()

    def step_b(j):
        @pl.when(even & low2)
        def _():
            @pl.when(high2)
            def _():
                term(j, 3, 0, {"ctx": p + 2}).wait_recv()
                acc[j, 1] += arrived[j, 0].astype(F32)

            terms[j, 1] = acc[j, 1].astype(BF16)
            term(j, 1, 1, {"ctx": p + 1}).start()

    def step_c(j):
        @pl.when(low2)
        def _():
            term(j, 3, 1, {"ctx": mate}).wait_recv()
            terms[j, 2] = (acc[j, 2] + arrived[j, 1].astype(F32)).astype(BF16)
            term(j, 2, 3, {"ctx": p - 2}).start()

    def step_d(j):
        @pl.when(even)
        def _():
            term(j, 1, 2, {"ctx": p + 1}).wait_recv()
            acc[j, 0] += arrived[j, 2].astype(F32)

        @pl.when(high2)
        def _():
            term(j, 2, 3, {"ctx": p + 2}).wait_recv()
            acc[j, 0] += arrived[j, 3].astype(F32)

        fsend[j] = acc[j, 0].astype(fsend.dtype)
        for k in range(1, tp):
            fin_copy(j, k).start()
        final[t, j] = fsend[j, :, my_rows]

    deltas = []
    stores = []

    def store(src, dst):
        copy = pltpu.make_async_copy(src, dst, out_sem.at[len(stores)])
        copy.start()
        stores.append(copy)

    for j in range(groups):
        pl.when(p >= 3)(lambda: slab(j, 2, 2, 3, {"ctx": mate}).wait_recv())
        scores(j, 3)
        out_t = forward(j)
        for k in range(1, tp):
            out_copy(j, k).start()
        cols = lanes(t * width + j * gw, gw)
        store(outs.at[my_rows, pl.ds(j * gw, gw)], attn_ref.at[:, cols])
        for k in range(1, tp):
            grad_copy(j, k).wait_recv()
        deltas.append(delta_of(j, out_t))
    for j in range(groups):
        backward(j, 3, deltas[j], True)
        step_a3(j)
    for j in range(groups):
        backward(j, 1, deltas[j], False)
        step_a1(j)
    for j in range(groups):
        step_b(j)
        backward(j, 2, deltas[j], False)
    for j in range(groups):
        backward(j, 0, deltas[j], False)
        step_c(j)
    for j in range(groups):
        finish_query(j)
    for j in range(groups):
        step_d(j)

    for j in range(groups):
        for k in range(1, tp):
            fin_copy(j, k).wait_recv()
    for head_group in range(KVH):
        owner, j = head_group * sharing // groups, head_group % groups
        both = final[owner, j].astype(F32)
        for s in range(1, sharing):
            both = both + final[owner + s, j].astype(F32)
        cols = pl.ds(head_group * HD, HD)
        kv_held[0, :, cols] = both[0].astype(BF16)
        kv_held[1, :, cols] = both[1].astype(BF16)
    store(kv_held.at[0], dk_ref)
    store(kv_held.at[1], dv_ref)

    for j in range(groups):
        for k in range(1, tp):
            grad_copy(j, k).wait_send()
            out_copy(j, k).wait_send()
            out_copy(j, k).wait_recv()
            fin_copy(j, k).wait_send()
        pl.when(high2)(lambda: slab(j, 0, 0, 2, {"ctx": p + 2}).wait_send())
        pl.when(even)(lambda: slab(j, 1, 0, 1, {"ctx": p + 1}).wait_send())
        pl.when(low2)(lambda: slab(j, 2, 2, 3, {"ctx": mate}).wait_send())
        pl.when(even & low2 & high2)(lambda: slab(j, 3, 1, 3, {"ctx": p + 2}).wait_send())
        pl.when(p >= 3)(lambda: term(j, 3, 0, {"ctx": mate}).wait_send())
        pl.when(p >= 1)(lambda: term(j, 1, 2, {"ctx": mate}).wait_send())
        pl.when(low2)(lambda: term(j, 2, 3, {"ctx": p - 2}).wait_send())
    for copy in stores:
        copy.wait()


def write_out(*refs):
    sources, targets, sems = refs[:4], refs[4:8], refs[8]
    copies = [pltpu.make_async_copy(sources[i], targets[i], sems.at[i]) for i in range(4)]
    for copy in copies:
        copy.start()
    for copy in copies:
        copy.wait()


def local(ctx, tp, query_heads, key_heads, value_heads, grad_rows, doc_lengths):
    tokens, width = query_heads.shape
    rows = grad_rows.shape[0]
    heads_dev = width // HD
    per_kv = H // KVH
    groups = max(1, heads_dev // per_kv)
    sharing = max(1, per_kv // heads_dev)
    per = heads_dev // groups
    final_type = BF16 if sharing == 1 else F32
    hbm = pl.BlockSpec(memory_space=pltpu.HBM)
    limit = 62 * 1024 * 1024
    dma = pltpu.SemaphoreType.DMA
    pair = (2, tokens, HD)
    results = pl.pallas_call(
        functools.partial(kernel, (ctx, tp, groups, per, sharing)),
        out_shape=(
            jax.ShapeDtypeStruct((rows, H * HD), BF16),
            jax.ShapeDtypeStruct((tokens, width), BF16),
            jax.ShapeDtypeStruct((rows, KVH * HD), BF16),
            jax.ShapeDtypeStruct((rows, KVH * HD), BF16),
        ),
        in_specs=[pl.BlockSpec(memory_space=pltpu.SMEM)] + [hbm] * 4,
        out_specs=(hbm,) * 4,
        scratch_shapes=[
            pltpu.VMEM((groups, SLOTS) + pair, BF16),
            pltpu.VMEM((tokens, width), BF16),
            pltpu.VMEM((groups, per * tokens, HD), BF16),
            pltpu.VMEM((groups, per * tokens, HD), BF16),
            pltpu.VMEM((SLOTS * tokens, tokens), F32),
            pltpu.VMEM((groups, SLOTS, tokens, per * tokens), F32),
            pltpu.VMEM((groups, HD, per * tokens), F32),
            pltpu.VMEM((tokens, width), BF16),
            pltpu.VMEM((groups, SLOTS) + pair, F32),
            pltpu.VMEM((groups, SLOTS) + pair, BF16),
            pltpu.VMEM((groups, SLOTS) + pair, BF16),
            pltpu.VMEM((groups,) + pair, final_type),
            pltpu.VMEM((tp, groups, 2, rows, HD), final_type),
            dma((groups, 4)),
            dma((groups, SLOTS)),
            dma((groups, tp)),
            dma((groups, tp)),
            dma((groups, tp)),
            dma((groups, tp)),
            dma((groups, SLOTS)),
            dma((groups, SLOTS)),
            dma((groups, tp)),
            dma((groups, tp)),
            dma((2 * groups + 1 + groups * per,)),
            pltpu.VMEM((tokens, width), BF16),
            pltpu.VMEM((2, rows, KVH * HD), BF16),
            dma((2 * groups + 2,)),
        ],
        compiler_params=pltpu.CompilerParams(
            collective_id=0, has_side_effects=True, vmem_limit_bytes=limit
        ),
    )(doc_lengths, query_heads, key_heads, value_heads, grad_rows)
    return pl.pallas_call(
        write_out,
        out_shape=tuple(jax.ShapeDtypeStruct(r.shape, r.dtype) for r in results),
        in_specs=[hbm] * 4,
        out_specs=(hbm,) * 4,
        scratch_shapes=[dma((4,))],
        compiler_params=pltpu.CompilerParams(vmem_limit_bytes=limit),
    )(*results)


def solution(mesh):
    return jax.shard_map(
        functools.partial(local, mesh.shape["ctx"], mesh.shape["tp"]),
        mesh=mesh,
        in_specs=(P("ctx", "tp"), P("ctx", None), P("ctx", None), P(("ctx", "tp"), None), P()),
        out_specs=(
            P(("ctx", "tp"), None),
            P("ctx", "tp"),
            P(("ctx", "tp"), None),
            P(("ctx", "tp"), None),
        ),
        check_vma=False,
    )
```

```python
import functools
import math

import jax
import jax.numpy as jnp
from jax import lax
from jax.experimental import pallas as pl
from jax.experimental.pallas import tpu as pltpu
from jax.sharding import PartitionSpec as P

H = 32
KVH = 8
HD = 128
BLK = 128
SLOTS = 4
NEG = -1e30
NT = (((1,), (1,)), ((), ()))
F32 = jnp.float32
BF16 = jnp.bfloat16


def kernel(
    dims,
    docs_ref,
    q_ref,
    k_ref,
    v_ref,
    g_ref,
    attn_ref,
    dq_ref,
    dk_ref,
    dv_ref,
    win,
    grads,
    q_all,
    g_all,
    bias,
    probs,
    dq_sum,
    outs,
    acc,
    terms,
    arrived,
    fsend,
    final,
    win_send,
    win_recv,
    g_send,
    g_recv,
    o_send,
    o_recv,
    r_send,
    r_recv,
    f_send,
    f_recv,
    in_sem,
    dq_held,
    kv_held,
    out_sem,
):
    ctx, tp, groups, per, sharing = dims
    tokens = q_ref.shape[0]
    rows = g_ref.shape[0]
    width = groups * per * HD
    gw = per * HD
    scaling = 1.0 / math.sqrt(HD)
    p = lax.axis_index("ctx")
    t = lax.axis_index("tp")
    even = lax.rem(p, 2) == 0
    odd = jnp.logical_not(even)
    mate = jnp.where(even, p + 1, p - 1)
    low2 = p >= 2
    high2 = p + 2 < ctx
    first_group = t * (groups * per) // (H // KVH)
    my_rows = pl.ds(pl.multiple_of(t * rows, rows), rows)

    def lanes(start, size):
        return pl.ds(pl.multiple_of(start, HD), size)

    barrier = pltpu.get_barrier_semaphore()

    def greet(device):
        pl.semaphore_signal(barrier, inc=1, device_id=device, device_id_type=pl.DeviceIdType.MESH)

    for k in range(1, tp):
        greet({"tp": lax.rem(t + k, tp)})
    greet({"ctx": mate})
    pl.when(low2)(lambda: greet({"ctx": p - 2}))
    pl.when(high2)(lambda: greet({"ctx": p + 2}))
    loads = []

    def load(src, dst):
        copy = pltpu.make_async_copy(src, dst, in_sem.at[len(loads)])
        copy.start()
        loads.append(copy)

    for j in range(groups):
        cols = lanes((first_group + j) * HD, HD)
        load(k_ref.at[:, cols], win.at[j, 0, 0])
        load(v_ref.at[:, cols], win.at[j, 0, 1])
    load(g_ref.at[:, lanes(t * width, width)], grads.at[my_rows])
    for j in range(groups):
        for i in range(per):
            load(
                q_ref.at[:, pl.ds((j * per + i) * HD, HD)],
                q_all.at[j, pl.ds(i * tokens, tokens)],
            )
    for copy in loads[: 2 * groups]:
        copy.wait()
    pl.semaphore_wait(barrier, tp + jnp.where(low2, 1, 0) + jnp.where(high2, 1, 0))

    def remote(src, dst, send, recv, device):
        return pltpu.make_async_remote_copy(
            src_ref=src,
            dst_ref=dst,
            send_sem=send,
            recv_sem=recv,
            device_id=device,
            device_id_type=pl.DeviceIdType.MESH,
        )

    def slab(j, kind, source, slot, device):
        return remote(
            win.at[j, source], win.at[j, slot], win_send.at[j, kind], win_recv.at[j, slot], device
        )

    def grad_copy(j, k):
        peer = lax.rem(t + k, tp)
        return remote(
            g_ref.at[:, lanes(peer * width + j * gw, gw)],
            grads.at[my_rows, pl.ds(j * gw, gw)],
            g_send.at[j, k],
            g_recv.at[j, k],
            {"tp": peer},
        )

    for j in range(groups):
        pl.when(high2)(lambda: slab(j, 0, 0, 2, {"ctx": p + 2}).start())
        pl.when(even)(lambda: slab(j, 1, 0, 1, {"ctx": p + 1}).start())
        for k in range(1, tp):
            grad_copy(j, k).start()

    for d in range(1, SLOTS):

        @pl.when(p < d)
        def _(d=d):
            for j in range(groups):
                win[j, d] = jnp.zeros(win.shape[2:], BF16)

    blocks = tokens // BLK
    ends = []
    total = jnp.int32(0)
    for i in range(docs_ref.shape[0]):
        total = total + docs_ref[i]
        ends.append(total)

    def doc_of(block):
        count = jnp.int32(0)
        for end in ends:
            count = count + jnp.where(end <= block, 1, 0)
        return jnp.where(block >= 0, count, -1)

    causal = lax.broadcasted_iota(jnp.int32, (BLK, BLK), 0) <= lax.broadcasted_iota(
        jnp.int32, (BLK, BLK), 1
    )
    query_docs = [doc_of(p * blocks + b) for b in range(blocks)]
    for d in range(SLOTS):
        for kb in range(blocks):
            key_doc = query_docs[kb] if d == 0 else doc_of((p - d) * blocks + kb)
            for qb in range(blocks):
                if d == 0 and kb > qb:
                    tile = jnp.full((BLK, BLK), NEG, F32)
                elif d == 0 and kb == qb:
                    tile = jnp.where(causal, 0.0, NEG).astype(F32)
                else:
                    level = jnp.where(key_doc == query_docs[qb], 0.0, NEG).astype(F32)
                    tile = jnp.full((BLK, BLK), level, F32)
                bias[pl.ds(d * tokens + kb * BLK, BLK), pl.ds(qb * BLK, BLK)] = tile

    for copy in loads[2 * groups :]:
        copy.wait()

    def scores(j, d):
        wide = lax.dot_general(win[j, d, 0], q_all[j], NT, preferred_element_type=F32)
        tile = bias[pl.ds(d * tokens, tokens), :]
        probs[j, d] = wide * scaling + jnp.concatenate([tile] * per, axis=1)

    for j in range(groups):

        @pl.when(low2)
        def _(j=j):
            slab(j, 0, 0, 2, {"ctx": p - 2}).wait_recv()
            pl.when(even)(lambda: slab(j, 2, 2, 3, {"ctx": p + 1}).start())
            pl.when(odd)(lambda: slab(j, 2, 2, 1, {"ctx": p - 1}).start())

    for j in range(groups):
        scores(j, 0)
    for j in range(groups):
        pl.when(p >= 1)(lambda: slab(j, 0, 0, 1, {"ctx": mate}).wait_recv())
        pl.when(even & low2 & high2)(lambda: slab(j, 3, 1, 3, {"ctx": p + 2}).start())

    for j in range(groups):
        scores(j, 2)
    for j in range(groups):
        scores(j, 1)

    def across(value):
        return value.astype(F32).T

    def forward(j):
        top = jnp.max(probs[j, 0], axis=0, keepdims=True)
        for d in range(1, SLOTS):
            top = jnp.maximum(top, jnp.max(probs[j, d], axis=0, keepdims=True))
        norm = jnp.zeros_like(top)
        for d in range(SLOTS):
            e = jnp.exp(probs[j, d] - top)
            probs[j, d] = e
            norm = norm + jnp.sum(e, axis=0, keepdims=True)
        inverse = 1.0 / norm
        out_t = jnp.zeros((HD, per * tokens), F32)
        for d in range(SLOTS):
            prob = probs[j, d] * inverse
            probs[j, d] = prob
            vals_t = across(win[j, d, 1]).astype(BF16)
            out_t = out_t + jnp.dot(vals_t, prob.astype(BF16), preferred_element_type=F32)
        out_t = out_t.astype(BF16).astype(F32)
        rows_of = out_t.T.astype(BF16)
        for i in range(per):
            cols = pl.ds((j * per + i) * HD, HD)
            outs[:, cols] = rows_of[i * tokens : (i + 1) * tokens]
        return out_t

    def delta_of(j, out_t):
        for i in range(per):
            cols = pl.ds((j * per + i) * HD, HD)
            g_all[j, pl.ds(i * tokens, tokens)] = grads[:, cols]
        return jnp.sum(across(g_all[j]) * out_t, axis=0, keepdims=True)

    def backward(j, d, delta, first):
        d_prob = lax.dot_general(win[j, d, 1], g_all[j], NT, preferred_element_type=F32)
        prob = probs[j, d]
        d_score = (prob * (d_prob - delta)).astype(BF16)
        keys_t = across(win[j, d, 0]).astype(BF16)
        dq_t = jnp.dot(keys_t, d_score, preferred_element_type=F32)
        dq_sum[j] = dq_t if first else dq_sum[j] + dq_t
        acc[j, d, 0] = jnp.dot(d_score, q_all[j], preferred_element_type=F32) * scaling
        acc[j, d, 1] = jnp.dot(prob.astype(BF16), g_all[j], preferred_element_type=F32)

    def finish_query(j):
        rows_of = (dq_sum[j] * scaling).T.astype(BF16)
        for i in range(per):
            cols = pl.ds((j * per + i) * HD, HD)
            dq_held[:, cols] = rows_of[i * tokens : (i + 1) * tokens]
        cols = pl.ds(j * gw, gw)
        store(dq_held.at[:, cols], dq_ref.at[:, cols])

    def term(j, kind, place, device):
        return remote(
            terms.at[j, kind], arrived.at[j, place], r_send.at[j, kind], r_recv.at[j, place], device
        )

    def out_copy(j, k):
        peer = lax.rem(t + k, tp)
        return remote(
            outs.at[pl.ds(pl.multiple_of(peer * rows, rows), rows), pl.ds(j * gw, gw)],
            attn_ref.at[:, lanes(t * width + j * gw, gw)],
            o_send.at[j, k],
            o_recv.at[j, k],
            {"tp": peer},
        )

    def fin_copy(j, k):
        peer = lax.rem(t + k, tp)
        return remote(
            fsend.at[j, :, pl.ds(pl.multiple_of(peer * rows, rows), rows)],
            final.at[t, j],
            f_send.at[j, k],
            f_recv.at[j, k],
            {"tp": peer},
        )

    def step_a3(j):
        @pl.when(p >= 3)
        def _():
            terms[j, 3] = acc[j, 3].astype(BF16)
            pl.when(even)(lambda: term(j, 3, 0, {"ctx": p - 2}).start())
            pl.when(odd)(lambda: term(j, 3, 1, {"ctx": p - 1}).start())

    def step_a1(j):
        @pl.when(odd)
        def _():
            terms[j, 1] = acc[j, 1].astype(BF16)
            term(j, 1, 2, {"ctx": p - 1}).start()

    def step_b(j):
        @pl.when(even & low2)
        def _():
            @pl.when(high2)
            def _():
                term(j, 3, 0, {"ctx": p + 2}).wait_recv()
                acc[j, 1] += arrived[j, 0].astype(F32)

            terms[j, 1] = acc[j, 1].astype(BF16)
            term(j, 1, 1, {"ctx": p + 1}).start()

    def step_c(j):
        @pl.when(low2)
        def _():
            term(j, 3, 1, {"ctx": mate}).wait_recv()
            terms[j, 2] = (acc[j, 2] + arrived[j, 1].astype(F32)).astype(BF16)
            term(j, 2, 3, {"ctx": p - 2}).start()

    def step_d(j):
        @pl.when(even)
        def _():
            term(j, 1, 2, {"ctx": p + 1}).wait_recv()
            acc[j, 0] += arrived[j, 2].astype(F32)

        @pl.when(high2)
        def _():
            term(j, 2, 3, {"ctx": p + 2}).wait_recv()
            acc[j, 0] += arrived[j, 3].astype(F32)

        fsend[j] = acc[j, 0].astype(fsend.dtype)
        for k in range(1, tp):
            fin_copy(j, k).start()
        final[t, j] = fsend[j, :, my_rows]

    deltas = []
    stores = []

    def store(src, dst):
        copy = pltpu.make_async_copy(src, dst, out_sem.at[len(stores)])
        copy.start()
        stores.append(copy)

    for j in range(groups):
        pl.when(p >= 3)(lambda: slab(j, 2, 2, 3, {"ctx": mate}).wait_recv())
        scores(j, 3)
        out_t = forward(j)
        for k in range(1, tp):
            out_copy(j, k).start()
        cols = lanes(t * width + j * gw, gw)
        store(outs.at[my_rows, pl.ds(j * gw, gw)], attn_ref.at[:, cols])
        for k in range(1, tp):
            grad_copy(j, k).wait_recv()
        deltas.append(delta_of(j, out_t))
    for j in range(groups):
        backward(j, 3, deltas[j], True)
        step_a3(j)
    for j in range(groups):
        backward(j, 1, deltas[j], False)
        step_a1(j)
    for j in range(groups):
        step_b(j)
        backward(j, 2, deltas[j], False)
    for j in range(groups):
        backward(j, 0, deltas[j], False)
        step_c(j)
    for j in range(groups):
        finish_query(j)
    for j in range(groups):
        step_d(j)

    for j in range(groups):
        for k in range(1, tp):
            fin_copy(j, k).wait_recv()
    for head_group in range(KVH):
        owner, j = head_group * sharing // groups, head_group % groups
        both = final[owner, j].astype(F32)
        for s in range(1, sharing):
            both = both + final[owner + s, j].astype(F32)
        cols = pl.ds(head_group * HD, HD)
        kv_held[0, :, cols] = both[0].astype(BF16)
        kv_held[1, :, cols] = both[1].astype(BF16)
    store(kv_held.at[0], dk_ref)
    store(kv_held.at[1], dv_ref)

    for j in range(groups):
        for k in range(1, tp):
            grad_copy(j, k).wait_send()
            out_copy(j, k).wait_send()
            out_copy(j, k).wait_recv()
            fin_copy(j, k).wait_send()
        pl.when(high2)(lambda: slab(j, 0, 0, 2, {"ctx": p + 2}).wait_send())
        pl.when(even)(lambda: slab(j, 1, 0, 1, {"ctx": p + 1}).wait_send())
        pl.when(low2)(lambda: slab(j, 2, 2, 3, {"ctx": mate}).wait_send())
        pl.when(even & low2 & high2)(lambda: slab(j, 3, 1, 3, {"ctx": p + 2}).wait_send())
        pl.when(p >= 3)(lambda: term(j, 3, 0, {"ctx": mate}).wait_send())
        pl.when(p >= 1)(lambda: term(j, 1, 2, {"ctx": mate}).wait_send())
        pl.when(low2)(lambda: term(j, 2, 3, {"ctx": p - 2}).wait_send())
    for copy in stores:
        copy.wait()


def write_out(*refs):
    sources, targets, held, sems = refs[:4], refs[4:8], refs[8:12], refs[12]
    reads = [pltpu.make_async_copy(sources[i], held[i], sems.at[0, i]) for i in range(4)]
    writes = [pltpu.make_async_copy(held[i], targets[i], sems.at[1, i]) for i in range(4)]
    for copy in reads:
        copy.start()
    for read, write in zip(reads, writes):
        read.wait()
        write.start()
    for copy in writes:
        copy.wait()


def local(ctx, tp, query_heads, key_heads, value_heads, grad_rows, doc_lengths):
    tokens, width = query_heads.shape
    rows = grad_rows.shape[0]
    heads_dev = width // HD
    per_kv = H // KVH
    groups = max(1, heads_dev // per_kv)
    sharing = max(1, per_kv // heads_dev)
    per = heads_dev // groups
    final_type = BF16 if sharing == 1 else F32
    hbm = pl.BlockSpec(memory_space=pltpu.HBM)
    limit = 62 * 1024 * 1024
    dma = pltpu.SemaphoreType.DMA
    pair = (2, tokens, HD)
    results = pl.pallas_call(
        functools.partial(kernel, (ctx, tp, groups, per, sharing)),
        out_shape=(
            jax.ShapeDtypeStruct((rows, H * HD), BF16),
            jax.ShapeDtypeStruct((tokens, width), BF16),
            jax.ShapeDtypeStruct((rows, KVH * HD), BF16),
            jax.ShapeDtypeStruct((rows, KVH * HD), BF16),
        ),
        in_specs=[pl.BlockSpec(memory_space=pltpu.SMEM)] + [hbm] * 4,
        out_specs=(hbm,) * 4,
        scratch_shapes=[
            pltpu.VMEM((groups, SLOTS) + pair, BF16),
            pltpu.VMEM((tokens, width), BF16),
            pltpu.VMEM((groups, per * tokens, HD), BF16),
            pltpu.VMEM((groups, per * tokens, HD), BF16),
            pltpu.VMEM((SLOTS * tokens, tokens), F32),
            pltpu.VMEM((groups, SLOTS, tokens, per * tokens), F32),
            pltpu.VMEM((groups, HD, per * tokens), F32),
            pltpu.VMEM((tokens, width), BF16),
            pltpu.VMEM((groups, SLOTS) + pair, F32),
            pltpu.VMEM((groups, SLOTS) + pair, BF16),
            pltpu.VMEM((groups, SLOTS) + pair, BF16),
            pltpu.VMEM((groups,) + pair, final_type),
            pltpu.VMEM((tp, groups, 2, rows, HD), final_type),
            dma((groups, 4)),
            dma((groups, SLOTS)),
            dma((groups, tp)),
            dma((groups, tp)),
            dma((groups, tp)),
            dma((groups, tp)),
            dma((groups, SLOTS)),
            dma((groups, SLOTS)),
            dma((groups, tp)),
            dma((groups, tp)),
            dma((2 * groups + 1 + groups * per,)),
            pltpu.VMEM((tokens, width), BF16),
            pltpu.VMEM((2, rows, KVH * HD), BF16),
            dma((2 * groups + 2,)),
        ],
        compiler_params=pltpu.CompilerParams(
            collective_id=0, has_side_effects=True, vmem_limit_bytes=limit
        ),
    )(doc_lengths, query_heads, key_heads, value_heads, grad_rows)
    return pl.pallas_call(
        write_out,
        out_shape=tuple(jax.ShapeDtypeStruct(r.shape, r.dtype) for r in results),
        in_specs=[hbm] * 4,
        out_specs=(hbm,) * 4,
        scratch_shapes=[pltpu.VMEM(r.shape, r.dtype) for r in results] + [dma((2, 4))],
        compiler_params=pltpu.CompilerParams(vmem_limit_bytes=limit),
    )(*results)


def solution(mesh):
    return jax.shard_map(
        functools.partial(local, mesh.shape["ctx"], mesh.shape["tp"]),
        mesh=mesh,
        in_specs=(P("ctx", "tp"), P("ctx", None), P("ctx", None), P(("ctx", "tp"), None), P()),
        out_specs=(
            P(("ctx", "tp"), None),
            P("ctx", "tp"),
            P(("ctx", "tp"), None),
            P(("ctx", "tp"), None),
        ),
        check_vma=False,
    )
```
